512 devices in a mesh: src: 32 (over z_lo, x, core), tgt: 16 (over z_hi, y).
Axes of the slice: x: 4, y: 8, z: 8 (z_hi: 2, z_lo: 4; z = z_hi * 4 + z_lo), core: 2. Of those that a mesh axis runs over, the one named last changes fastest.
Arguments:
- src_embed: bfloat16 [8192, 1024], P('src', 'tgt'), as said below
- tgt_embed: bfloat16 [4096, 1024], P('tgt', 'src')
- src_near: int32 [8192, 16], P('src'), may hold values from 0 to 4095
- tgt_near: int32 [4096, 16], P('tgt'), may hold values from 0 to 8191
Outputs:
- margin: bfloat16 [8192, 4096], P('src', 'tgt')
- src_average: float32 [8192], P('src')
- tgt_average: float32 [4096], P('tgt')
The draws below stay inside these ranges and needn't reach their ends.
Inputs may be any that keep to these rules, and one draw needn't show every extreme that they name: `src_embed`: every embedding is a sentence-specific multiple of one direction shared by both languages plus independent variation of comparable size, so that all cosines of the draw are positive.
All inputs are finite; a program needn't handle non-finite values.
Results may differ from the reference program's by a relative error of at most 0.001.
Values may be sent and summed in bfloat16 or wider, within the bound.
No kernel may reach another device: no remote copies, remote signals or barrier semaphores. Data moves between devices by JAX's collectives and lax.ppermute only.
A program may use at most 64 MiB of HBM per device.

```python
import jax
import jax.numpy as jnp
from jax import lax

D = 1024
K = 16
RS = 256
RT = 256
NS = 8192
NT = 4096


def shared_direction(key):
    return jax.random.normal(key, (D,), jnp.float32)


def embed_rows(key, count, direction):
    key_scale, key_noise = jax.random.split(key)
    scales = jnp.exp(jax.random.uniform(key_scale, (count, 1), jnp.float32, jnp.log(0.5), jnp.log(4.0)))
    noise = jnp.clip(jax.random.normal(key_noise, (count, D), jnp.float32), -6.0, 6.0)
    return (scales * direction[None, :] + noise).astype(jnp.bfloat16)


def draw_src_embed(key, part):
    direction = shared_direction(key)
    key = jax.random.fold_in(key, 11)
    return embed_rows(key, NS, direction)


def draw_tgt_embed(key, part):
    direction = shared_direction(key)
    key = jax.random.fold_in(key, 23)
    return embed_rows(key, NT, direction)


def with_ends(drawn, own_key, low, high):
    dims = drawn.shape
    place = [jax.random.randint(jax.random.fold_in(own_key, axis), (), 0, dims[axis]) for axis in range(len(dims))]
    drawn = drawn.at[tuple(place)].set(low)
    longest = dims.index(max(dims))
    place[longest] = (place[longest] + 1) % dims[longest]
    return drawn.at[tuple(place)].set(high)


def setup_inputs(seed: int = 0) -> dict:
    key_of = jax.random.split(jax.random.key(seed), 5)
    return {
        "src_embed": draw_src_embed(jax.random.fold_in(key_of[4], 71), 0),
        "tgt_embed": draw_tgt_embed(jax.random.fold_in(key_of[4], 71), 0),
        "src_near": with_ends(jax.random.randint(key_of[2], (NS, K), 0, NT), jax.random.fold_in(key_of[2], 1), 0, NT - 1).astype(jnp.int32),
        "tgt_near": with_ends(jax.random.randint(key_of[3], (NT, K), 0, NS), jax.random.fold_in(key_of[3], 1), 0, NS - 1).astype(jnp.int32),
    }


EPSILON = 1e-06

def row_norms(values):
    wide = values.astype(jnp.float32)
    return jnp.sqrt(lax.optimization_barrier(jnp.sum(wide * wide, axis=1)) + EPSILON)

def reference(src_embed, tgt_embed, src_near, tgt_near):
    src_wide = src_embed.astype(jnp.float32)
    tgt_wide = tgt_embed.astype(jnp.float32)
    src_norm = row_norms(src_embed)
    tgt_norm = row_norms(tgt_embed)

    def src_block(index):
        start = (index * RS).astype(jnp.int32)
        rows = lax.dynamic_slice_in_dim(src_wide, start, RS, 0)
        near = lax.dynamic_slice_in_dim(src_near, start, RS, 0)
        norms = lax.dynamic_slice_in_dim(src_norm, start, RS, 0)
        partner = tgt_wide[near]
        dots = jnp.einsum('rd,rkd->rk', rows, partner, precision=lax.Precision.HIGHEST)
        cosines = dots / (norms[:, None] * tgt_norm[near])
        return lax.optimization_barrier(jnp.sum(cosines, axis=1)) / K
    src_average = lax.map(src_block, jnp.arange(NS // RS, dtype=jnp.int32)).reshape(NS)

    def tgt_block(index):
        start = (index * RT).astype(jnp.int32)
        rows = lax.dynamic_slice_in_dim(tgt_wide, start, RT, 0)
        near = lax.dynamic_slice_in_dim(tgt_near, start, RT, 0)
        norms = lax.dynamic_slice_in_dim(tgt_norm, start, RT, 0)
        partner = src_wide[near]
        dots = jnp.einsum('rd,rkd->rk', rows, partner, precision=lax.Precision.HIGHEST)
        cosines = dots / (norms[:, None] * src_norm[near])
        return lax.optimization_barrier(jnp.sum(cosines, axis=1)) / K
    tgt_average = lax.map(tgt_block, jnp.arange(NT // RT, dtype=jnp.int32)).reshape(NT)

    def margin_block(index):
        start = (index * RS).astype(jnp.int32)
        rows = lax.dynamic_slice_in_dim(src_wide, start, RS, 0)
        norms = lax.dynamic_slice_in_dim(src_norm, start, RS, 0)
        means = lax.dynamic_slice_in_dim(src_average, start, RS, 0)
        dots = jnp.dot(rows, tgt_wide.T, precision=lax.Precision.HIGHEST)
        cosines = dots / (norms[:, None] * tgt_norm[None, :])
        return (cosines / ((means[:, None] + tgt_average[None, :]) / 2.0)).astype(jnp.bfloat16)
    margin = lax.map(margin_block, jnp.arange(NS // RS, dtype=jnp.int32)).reshape(NS, NT)
    return (margin, src_average, tgt_average)
```

```python
import jax
import jax.numpy as jnp
from jax import lax
from jax.experimental import pallas as pl
from jax.experimental.pallas import tpu as pltpu
from jax.sharding import PartitionSpec as P

EPSILON = 1e-06
LANES = 128
CORES = 2
MAJOR = (((0,), (0,)), ((), ()))


def spread(values, count):
    return jnp.broadcast_to(values[None], (count,) + values.shape)


def inverse_norms(values):
    wide = values.astype(jnp.float32)
    return lax.rsqrt(jnp.sum(wide * wide, axis=0, keepdims=True) + EPSILON)


def picked(cosines, index):
    total = jnp.zeros(index.shape, jnp.float32)
    for half in range(cosines.shape[1] // LANES):
        block = cosines[:, half * LANES : (half + 1) * LANES]
        found = jnp.take_along_axis(block, index & (LANES - 1), axis=1)
        total = total + jnp.where(index >> 7 == half, found, 0.0)
    return jnp.sum(total.T, axis=0, keepdims=True)


def tile_kernel(core_ref, s_ref, own_ref, other_ref, near_t_ref, near_s_ref, cos_ref, row_ref, col_ref):
    core = core_ref[0]
    parts, _, width, rows = s_ref.shape
    flat = (parts * width, rows)
    s_own = s_ref[:, pl.ds(core, 1)].reshape(flat)
    s_other = s_ref[:, pl.ds(1 - core, 1)].reshape(flat)
    t_own = own_ref[...].reshape(flat)
    t_other = other_ref[...].reshape(flat)
    s_scale = inverse_norms(jnp.concatenate([s_own, s_other], axis=0))
    t_scale = inverse_norms(jnp.concatenate([t_own, t_other], axis=0))

    def product(a, b):
        return lax.dot_general(a, b, MAJOR, preferred_element_type=jnp.float32)

    def column(scale):
        return jnp.broadcast_to(scale, (8, rows)).T[:, :1]

    cosines = product(s_own, t_own) + product(s_other, t_other)
    cosines = cosines * column(s_scale) * t_scale
    cos_ref[...] = cosines
    row_ref[...] = picked(cosines, near_t_ref[...])
    flipped = product(t_own, s_own) + product(t_other, s_other)
    flipped = flipped * column(t_scale) * s_scale
    col_ref[...] = picked(flipped, near_s_ref[...])


def local(src_embed, tgt_embed, src_near, tgt_near):
    src_index = lax.axis_index("src")
    tgt_index = lax.axis_index("tgt")
    core = src_index % CORES
    src_size = lax.axis_size("src")
    tgt_size = lax.axis_size("tgt")
    chips = src_size // CORES
    src_count, near_count = src_near.shape
    tgt_count = tgt_near.shape[0]
    pair = [(i, i ^ 1) for i in range(src_size)]
    same_core = [[q * CORES + c for q in range(chips)] for c in range(CORES)]

    def index_of(s, t):
        return s * tgt_size + t

    lines = [[index_of(q * CORES, t) for t in range(tgt_size)] for q in range(chips)]
    lines += [[index_of(q * CORES + 1, t) for q in range(chips)] for t in range(tgt_size)]

    def padded(near, start):
        return jnp.pad(near - start, ((0, 0), (0, LANES - near_count)), constant_values=-1)

    near_t = padded(src_near, tgt_index * tgt_count)
    near_s = padded(tgt_near, src_index * src_count)
    own = lax.all_to_all(
        spread(tgt_embed.T, chips), "src", 0, 0, axis_index_groups=same_core
    )
    own, src_part = lax.optimization_barrier((own, src_embed))
    other = lax.ppermute(own, "src", pair)
    source = lax.all_to_all(spread(src_part.T, tgt_size), "tgt", 0, 0)
    source = source.reshape(tgt_size, CORES, -1, src_count)
    vmem = pl.BlockSpec(memory_space=pltpu.VMEM)
    smem = pl.BlockSpec(memory_space=pltpu.SMEM)
    cosines, row, col = pl.pallas_call(
        tile_kernel,
        in_specs=[smem] + [vmem] * 5,
        out_specs=[vmem] * 3,
        out_shape=[
            jax.ShapeDtypeStruct((src_count, tgt_count), jnp.float32),
            jax.ShapeDtypeStruct((1, src_count), jnp.float32),
            jax.ShapeDtypeStruct((1, tgt_count), jnp.float32),
        ],
        compiler_params=pltpu.CompilerParams(vmem_limit_bytes=32 * 1024 * 1024),
        cost_estimate=pl.CostEstimate(flops=300_000_000, bytes_accessed=2**21, transcendentals=512),
    )(core.astype(jnp.int32).reshape(1), source, own, other, near_t, near_s)

    first = core == 0
    crossed = lax.ppermute(jnp.where(first, col, row), "src", pair)
    sums = jnp.where(
        first,
        jnp.concatenate([row, crossed], axis=0),
        jnp.broadcast_to(col + crossed, (2, tgt_count)),
    )
    parts = lax.all_to_all(spread(sums, chips), ("src", "tgt"), 0, 0, axis_index_groups=lines)
    averages = jnp.sum(parts, axis=0) / near_count
    kept = averages[0]
    crossed = lax.ppermute(averages[1], "src", pair)
    src_average = jnp.where(first, kept, crossed)
    tgt_average = jnp.where(first, crossed, kept)
    margin = (cosines / ((src_average[:, None] + tgt_average[None, :]) / 2.0)).astype(
        jnp.bfloat16
    )
    return (margin, src_average, tgt_average)


def solution(mesh):
    placed = (P("src", "tgt"), P("tgt", "src"), P("src", None), P("tgt", None))
    return jax.shard_map(
        local,
        mesh=mesh,
        in_specs=placed,
        out_specs=(P("src", "tgt"), P("src"), P("tgt")),
        check_vma=False,
    )
```

```python
import itertools

import jax
import jax.numpy as jnp
from jax import lax
from jax.experimental import pallas as pl
from jax.experimental.pallas import tpu as pltpu
from jax.sharding import PartitionSpec as P

EPSILON = 1e-06
LANES = 128
CORES = 2
ROW = 4
MAJOR = (((0,), (0,)), ((), ()))


def spread(values, count):
    return jnp.broadcast_to(values[None], (count,) + values.shape)


def inverse_norms(values):
    wide = values.astype(jnp.float32)
    return lax.rsqrt(jnp.sum(wide * wide, axis=0, keepdims=True) + EPSILON)


def picked(cosines, index):
    total = jnp.zeros(index.shape, jnp.float32)
    for half in range(cosines.shape[1] // LANES):
        block = cosines[:, half * LANES : (half + 1) * LANES]
        found = jnp.take_along_axis(block, index & (LANES - 1), axis=1)
        total = total + jnp.where(index >> 7 == half, found, 0.0)
    return jnp.sum(total.T, axis=0, keepdims=True)


def lanes_of(near, start):
    count, rows = near.shape
    fill = jnp.full((LANES - count, rows), -1, jnp.int32)
    return jnp.concatenate([near - start, fill], axis=0).T


def target_kernel(start_ref, t_ref, near_t_ref, near_s_ref, ordered_ref, scale_ref, lanes_t_ref, lanes_s_ref):
    cores, fars, planes, closes = t_ref.shape[:4]
    order = itertools.product(range(planes), range(fars), range(closes), range(cores))
    targets = jnp.concatenate([t_ref[c, far, p, close] for p, far, close, c in order], axis=0)
    ordered_ref[...] = targets
    scale_ref[...] = inverse_norms(targets)
    lanes_t_ref[...] = lanes_of(near_t_ref[...], start_ref[0])
    lanes_s_ref[...] = lanes_of(near_s_ref[...], start_ref[1])


def tile_kernel(s_ref, t_ref, scale_ref, lanes_t_ref, lanes_s_ref, cos_ref, row_ref, col_ref):
    sources = s_ref[...]
    targets = t_ref[...]
    s_scale = inverse_norms(sources)
    t_scale = scale_ref[...]

    def product(a, b):
        return lax.dot_general(a, b, MAJOR, preferred_element_type=jnp.float32)

    def column(scale):
        return jnp.broadcast_to(scale, (8, scale.shape[1])).T[:, :1]

    cosines = product(sources, targets) * column(s_scale) * t_scale
    cos_ref[...] = cosines
    row_ref[...] = picked(cosines, lanes_t_ref[...])
    flipped = product(targets, sources) * column(t_scale) * s_scale
    col_ref[...] = picked(flipped, lanes_s_ref[...])


def local(src_embed, tgt_embed, src_near, tgt_near):
    src_index = lax.axis_index("src")
    tgt_index = lax.axis_index("tgt")
    core = src_index % CORES
    src_size = lax.axis_size("src")
    tgt_size = lax.axis_size("tgt")
    chips = src_size // CORES
    src_count, near_count = src_near.shape
    tgt_count = tgt_near.shape[0]
    pairs = [[q * CORES + c for c in range(CORES)] for q in range(chips)]
    near_line = ROW // 2
    planes = chips // ROW

    def device(plane, far, close, c):
        return ((plane * 2 + far) * near_line + close) * CORES + c

    blocks = [
        [device(p, far, close, c) for p in range(planes) for close in range(near_line)]
        for far in range(2)
        for c in range(CORES)
    ]
    far_pairs = [
        [device(p, far, close, c) for far in range(2)]
        for p in range(planes)
        for close in range(near_line)
        for c in range(CORES)
    ]

    def index_of(s, t):
        return s * tgt_size + t

    lines = [[index_of(q * CORES, t) for t in range(tgt_size)] for q in range(chips)]
    lines += [[index_of(q * CORES + 1, t) for q in range(chips)] for t in range(tgt_size)]

    starts = jnp.stack([tgt_index * tgt_count, src_index * src_count]).astype(jnp.int32)
    own = lax.all_to_all(spread(tgt_embed.T, len(blocks[0])), "src", 0, 0, axis_index_groups=blocks)
    own, src_part = lax.optimization_barrier((own, src_embed))
    source = lax.all_to_all(spread(src_part.T, tgt_size), "tgt", 0, 0)
    source = source.reshape(-1, src_count)
    own = own.reshape(planes, near_line, -1, tgt_count)
    halves = lax.all_gather(own, "src", axis=0, axis_index_groups=far_pairs)
    halves = lax.all_gather(halves, "src", axis=0, axis_index_groups=pairs)
    smem = pl.BlockSpec(memory_space=pltpu.SMEM)
    vmem = pl.BlockSpec(memory_space=pltpu.VMEM)
    wide = (src_count, LANES)
    targets, scale, lanes_t, lanes_s = pl.pallas_call(
        target_kernel,
        in_specs=[smem] + [vmem] * 3,
        out_specs=[vmem] * 4,
        out_shape=[
            jax.ShapeDtypeStruct((source.shape[0], tgt_count), jnp.bfloat16),
            jax.ShapeDtypeStruct((1, tgt_count), jnp.float32),
            jax.ShapeDtypeStruct(wide, jnp.int32),
            jax.ShapeDtypeStruct((tgt_count, LANES), jnp.int32),
        ],
        compiler_params=pltpu.CompilerParams(vmem_limit_bytes=32 * 1024 * 1024),
        cost_estimate=pl.CostEstimate(flops=1_000_000, bytes_accessed=2**20, transcendentals=256),
    )(starts, halves, src_near.T, tgt_near.T)
    cosines, row, col = pl.pallas_call(
        tile_kernel,
        in_specs=[vmem] * 5,
        out_specs=[vmem] * 3,
        out_shape=[
            jax.ShapeDtypeStruct((src_count, tgt_count), jnp.float32),
            jax.ShapeDtypeStruct((1, src_count), jnp.float32),
            jax.ShapeDtypeStruct((1, tgt_count), jnp.float32),
        ],
        compiler_params=pltpu.CompilerParams(vmem_limit_bytes=32 * 1024 * 1024),
        cost_estimate=pl.CostEstimate(flops=300_000_000, bytes_accessed=2**21, transcendentals=512),
    )(source, targets, scale, lanes_t, lanes_s)

    first = core == 0
    both = lax.all_gather(
        jnp.concatenate([row, col], axis=0), "src", axis=0, axis_index_groups=pairs
    )
    sums = jnp.where(first, both[:, 0], jnp.broadcast_to(jnp.sum(both[:, 1], axis=0), (2, tgt_count)))
    parts = lax.all_to_all(spread(sums, chips), ("src", "tgt"), 0, 0, axis_index_groups=lines)
    averages = jnp.sum(parts, axis=0) / near_count
    both = lax.all_gather(averages, "src", axis=0, axis_index_groups=pairs)
    src_average = jnp.where(first, both[0, 0], both[0, 1])
    tgt_average = both[1, 0]
    margin = (cosines / ((src_average[:, None] + tgt_average[None, :]) / 2.0)).astype(
        jnp.bfloat16
    )
    return (margin, src_average, tgt_average)


def solution(mesh):
    placed = (P("src", "tgt"), P("tgt", "src"), P("src", None), P("tgt", None))
    return jax.shard_map(
        local,
        mesh=mesh,
        in_specs=placed,
        out_specs=(P("src", "tgt"), P("src"), P("tgt")),
        check_vma=False,
    )
```

```python
import itertools

import jax
import jax.numpy as jnp
from jax import lax
from jax.experimental import pallas as pl
from jax.experimental.pallas import tpu as pltpu
from jax.sharding import PartitionSpec as P

EPSILON = 1e-06
LANES = 128
CORES = 2
ROW = 4
MAJOR = (((0,), (0,)), ((), ()))


def spread(values, count):
    return jnp.broadcast_to(values[None], (count,) + values.shape)


def inverse_norms(values):
    wide = values.astype(jnp.float32)
    return lax.rsqrt(jnp.sum(wide * wide, axis=0, keepdims=True) + EPSILON)


def picked(cosines, index):
    total = jnp.zeros(index.shape, jnp.float32)
    for half in range(cosines.shape[1] // LANES):
        block = cosines[:, half * LANES : (half + 1) * LANES]
        found = jnp.take_along_axis(block, index & (LANES - 1), axis=1)
        total = total + jnp.where(index >> 7 == half, found, 0.0)
    return jnp.sum(total.T, axis=0, keepdims=True)


def lanes_of(near, start):
    count, rows = near.shape
    fill = jnp.full((LANES - count, rows), -1, jnp.int32)
    return jnp.concatenate([near - start, fill], axis=0).T


def target_kernel(start_ref, t_ref, near_t_ref, near_s_ref, ordered_ref, scale_ref, lanes_t_ref, lanes_s_ref):
    fars, cores, planes, closes = t_ref.shape[:4]
    order = itertools.product(range(planes), range(fars), range(closes), range(cores))
    pieces = [t_ref[far, c, p, close] for p, far, close, c in order]
    half = len(pieces) // 2
    targets = jnp.concatenate(
        [pieces[h * half + k + c] for k in range(0, half, cores) for h in range(2) for c in range(cores)], axis=0
    )
    ordered_ref[...] = targets
    scale_ref[...] = inverse_norms(targets)
    lanes_t_ref[...] = lanes_of(near_t_ref[...], start_ref[0])
    lanes_s_ref[...] = lanes_of(near_s_ref[...], start_ref[1])


def tile_kernel(s_ref, t_ref, scale_ref, lanes_t_ref, lanes_s_ref, cos_ref, row_ref, col_ref):
    sources = s_ref[...]
    targets = t_ref[...]
    s_scale = inverse_norms(sources)
    t_scale = scale_ref[...]

    def product(a, b):
        return lax.dot_general(a, b, MAJOR, preferred_element_type=jnp.float32)

    def column(scale):
        return jnp.broadcast_to(scale, (8, scale.shape[1])).T[:, :1]

    cosines = product(sources, targets) * column(s_scale) * t_scale
    cos_ref[...] = cosines
    row_ref[...] = picked(cosines, lanes_t_ref[...])
    flipped = product(targets, sources) * column(t_scale) * s_scale
    col_ref[...] = picked(flipped, lanes_s_ref[...])


def margin_kernel(core_ref, both_ref, cos_ref, margin_ref, src_ref, tgt_ref):
    src_average = both_ref[0, pl.ds(core_ref[0], 1)]
    tgt_average = both_ref[1, :1]
    src_ref[...] = src_average
    tgt_ref[...] = tgt_average
    rows = src_average.shape[1]
    column = jnp.broadcast_to(src_average, (8, rows)).T[:, :1]
    margin_ref[...] = (cos_ref[...] / ((column + tgt_average) / 2.0)).astype(jnp.bfloat16)


def local(src_embed, tgt_embed, src_near, tgt_near):
    src_index = lax.axis_index("src")
    tgt_index = lax.axis_index("tgt")
    core = src_index % CORES
    src_size = lax.axis_size("src")
    tgt_size = lax.axis_size("tgt")
    chips = src_size // CORES
    src_count, near_count = src_near.shape
    tgt_count = tgt_near.shape[0]
    pairs = [[q * CORES + c for c in range(CORES)] for q in range(chips)]
    line = tgt_size // 2
    layers = [[k, k + line] for k in range(line)]
    lines_y = [[h * line + k for k in range(line)] for h in range(2)]
    near_line = ROW // 2
    planes = chips // ROW

    def device(plane, far, close, c):
        return ((plane * 2 + far) * near_line + close) * CORES + c

    blocks = [
        [device(p, far, close, c) for p in range(planes) for close in range(near_line)]
        for far in range(2)
        for c in range(CORES)
    ]
    quads = [
        [device(p, far, close, c) for far in range(2) for c in range(CORES)]
        for p in range(planes)
        for close in range(near_line)
    ]

    def index_of(s, t):
        return s * tgt_size + t

    lines = [[index_of(q * CORES, t) for t in range(tgt_size)] for q in range(chips)]
    lines += [[index_of(q * CORES + 1, t) for q in range(chips)] for t in range(tgt_size)]

    starts = jnp.stack([tgt_index * tgt_count, src_index * src_count]).astype(jnp.int32)
    own = lax.all_to_all(spread(tgt_embed.T, len(blocks[0])), "src", 0, 0, axis_index_groups=blocks)
    src_part = lax.all_gather(src_embed.T, "tgt", axis=0, axis_index_groups=layers)
    own, src_part = lax.optimization_barrier((own, src_part))
    source = lax.all_to_all(spread(src_part, line), "tgt", 0, 0, axis_index_groups=lines_y)
    source = source.reshape(-1, src_count)
    own = own.reshape(planes, near_line, -1, tgt_count)
    halves = lax.all_gather(own, "src", axis=0, axis_index_groups=quads)
    halves = halves.reshape((2, CORES) + own.shape)
    smem = pl.BlockSpec(memory_space=pltpu.SMEM)
    vmem = pl.BlockSpec(memory_space=pltpu.VMEM)
    wide = (src_count, LANES)
    targets, scale, lanes_t, lanes_s = pl.pallas_call(
        target_kernel,
        in_specs=[smem] + [vmem] * 3,
        out_specs=[vmem] * 4,
        out_shape=[
            jax.ShapeDtypeStruct((source.shape[0], tgt_count), jnp.bfloat16),
            jax.ShapeDtypeStruct((1, tgt_count), jnp.float32),
            jax.ShapeDtypeStruct(wide, jnp.int32),
            jax.ShapeDtypeStruct((tgt_count, LANES), jnp.int32),
        ],
        compiler_params=pltpu.CompilerParams(vmem_limit_bytes=32 * 1024 * 1024),
        cost_estimate=pl.CostEstimate(flops=1_000_000, bytes_accessed=2**20, transcendentals=256),
    )(starts, halves, src_near.T, tgt_near.T)
    cosines, row, col = pl.pallas_call(
        tile_kernel,
        in_specs=[vmem] * 5,
        out_specs=[vmem] * 3,
        out_shape=[
            jax.ShapeDtypeStruct((src_count, tgt_count), jnp.float32),
            jax.ShapeDtypeStruct((1, src_count), jnp.float32),
            jax.ShapeDtypeStruct((1, tgt_count), jnp.float32),
        ],
        compiler_params=pltpu.CompilerParams(vmem_limit_bytes=32 * 1024 * 1024),
        cost_estimate=pl.CostEstimate(flops=300_000_000, bytes_accessed=2**21, transcendentals=512),
    )(source, targets, scale, lanes_t, lanes_s)

    first = core == 0
    both = lax.all_gather(
        jnp.concatenate([row, col], axis=0), "src", axis=0, axis_index_groups=pairs
    )
    sums = jnp.where(first, both[:, 0], jnp.broadcast_to(jnp.sum(both[:, 1], axis=0), (2, tgt_count)))
    parts = lax.all_to_all(spread(sums, chips), ("src", "tgt"), 0, 0, axis_index_groups=lines)
    averages = jnp.sum(parts, axis=0) / near_count
    both = lax.all_gather(averages, "src", axis=0, axis_index_groups=pairs)
    margin, src_average, tgt_average = pl.pallas_call(
        margin_kernel,
        in_specs=[smem] + [vmem] * 2,
        out_specs=[vmem] * 3,
        out_shape=[
            jax.ShapeDtypeStruct((src_count, tgt_count), jnp.bfloat16),
            jax.ShapeDtypeStruct((1, src_count), jnp.float32),
            jax.ShapeDtypeStruct((1, tgt_count), jnp.float32),
        ],
        compiler_params=pltpu.CompilerParams(vmem_limit_bytes=8 * 1024 * 1024),
        cost_estimate=pl.CostEstimate(flops=200_000, bytes_accessed=2**19, transcendentals=0),
    )(core.astype(jnp.int32).reshape(1), both, cosines)
    return (margin, src_average.reshape(src_count), tgt_average.reshape(tgt_count))


def solution(mesh):
    placed = (P("src", "tgt"), P("tgt", "src"), P("src", None), P("tgt", None))
    return jax.shard_map(
        local,
        mesh=mesh,
        in_specs=placed,
        out_specs=(P("src", "tgt"), P("src"), P("tgt")),
        check_vma=False,
    )
```

```python
import itertools

import jax
import jax.numpy as jnp
from jax import lax
from jax.experimental import pallas as pl
from jax.experimental.pallas import tpu as pltpu
from jax.sharding import PartitionSpec as P

EPSILON = 1e-06
LANES = 128
CORES = 2
ROW = 4
MAJOR = (((0,), (0,)), ((), ()))


def spread(values, count):
    return jnp.broadcast_to(values[None], (count,) + values.shape)


def inverse_norms(values):
    wide = values.astype(jnp.float32)
    return lax.rsqrt(jnp.sum(wide * wide, axis=0, keepdims=True) + EPSILON)


def picked(cosines, index):
    total = jnp.zeros(index.shape, jnp.float32)
    for half in range(cosines.shape[1] // LANES):
        block = cosines[:, half * LANES : (half + 1) * LANES]
        found = jnp.take_along_axis(block, index & (LANES - 1), axis=1)
        total = total + jnp.where(index >> 7 == half, found, 0.0)
    return jnp.sum(total.T, axis=0, keepdims=True)


def lanes_of(near, start):
    count, rows = near.shape
    fill = jnp.full((LANES - count, rows), -1, jnp.int32)
    return jnp.concatenate([near - start, fill], axis=0).T


def target_kernel(start_ref, t_ref, near_t_ref, near_s_ref, ordered_ref, scale_ref, lanes_t_ref, lanes_s_ref):
    fars, cores, planes, closes = t_ref.shape[:4]
    order = itertools.product(range(planes), range(fars), range(closes), range(cores))
    pieces = [t_ref[far, c, p, close] for p, far, close, c in order]
    half = len(pieces) // 2
    targets = jnp.concatenate(
        [pieces[h * half + k + c] for k in range(0, half, cores) for h in range(2) for c in range(cores)], axis=0
    )
    ordered_ref[...] = targets
    scale_ref[...] = inverse_norms(targets)
    lanes_t_ref[...] = lanes_of(near_t_ref[...], start_ref[0])
    lanes_s_ref[...] = lanes_of(near_s_ref[...], start_ref[1])


def tile_kernel(s_ref, t_ref, scale_ref, lanes_t_ref, lanes_s_ref, cos_ref, row_ref, col_ref):
    sources = s_ref[...]
    targets = t_ref[...]
    s_scale = inverse_norms(sources)

    column = jnp.broadcast_to(s_scale, (8, s_scale.shape[1])).T[:, :1]
    products = lax.dot_general(sources, targets, MAJOR, preferred_element_type=jnp.float32)
    cosines = products * column * scale_ref[...]
    cos_ref[...] = cosines
    row_ref[...] = picked(cosines, lanes_t_ref[...])
    col_ref[...] = picked(cosines.T, lanes_s_ref[...])


def margin_kernel(core_ref, both_ref, cos_ref, margin_ref, src_ref, tgt_ref):
    src_average = both_ref[0, pl.ds(core_ref[0], 1)]
    tgt_average = both_ref[1, :1]
    src_ref[...] = src_average
    tgt_ref[...] = tgt_average
    rows = src_average.shape[1]
    column = jnp.broadcast_to(src_average, (8, rows)).T[:, :1]
    margin_ref[...] = (cos_ref[...] / ((column + tgt_average) / 2.0)).astype(jnp.bfloat16)


def local(src_embed, tgt_embed, src_near, tgt_near):
    src_index = lax.axis_index("src")
    tgt_index = lax.axis_index("tgt")
    core = src_index % CORES
    src_size = lax.axis_size("src")
    tgt_size = lax.axis_size("tgt")
    chips = src_size // CORES
    src_count, near_count = src_near.shape
    tgt_count = tgt_near.shape[0]
    pairs = [[q * CORES + c for c in range(CORES)] for q in range(chips)]
    line = tgt_size // 2
    layers = [[k, k + line] for k in range(line)]
    lines_y = [[h * line + k for k in range(line)] for h in range(2)]
    near_line = ROW // 2
    planes = chips // ROW

    def device(plane, far, close, c):
        return ((plane * 2 + far) * near_line + close) * CORES + c

    blocks = [
        [device(p, far, close, c) for p in range(planes) for close in range(near_line)]
        for far in range(2)
        for c in range(CORES)
    ]
    quads = [
        [device(p, far, close, c) for far in range(2) for c in range(CORES)]
        for p in range(planes)
        for close in range(near_line)
    ]

    def index_of(s, t):
        return s * tgt_size + t

    lines = [[index_of(q * CORES, t) for t in range(tgt_size)] for q in range(chips)]
    lines += [[index_of(q * CORES + 1, t) for q in range(chips)] for t in range(tgt_size)]

    starts = jnp.stack([tgt_index * tgt_count, src_index * src_count]).astype(jnp.int32)
    own = lax.all_to_all(spread(tgt_embed.T, len(blocks[0])), "src", 0, 0, axis_index_groups=blocks)
    src_part = lax.all_gather(src_embed.T, "tgt", axis=0, axis_index_groups=layers)
    own, src_part = lax.optimization_barrier((own, src_part))
    source = lax.all_to_all(spread(src_part, line), "tgt", 0, 0, axis_index_groups=lines_y)
    source = source.reshape(-1, src_count)
    own = own.reshape(planes, near_line, -1, tgt_count)
    halves = lax.all_gather(own, "src", axis=0, axis_index_groups=quads)
    halves = halves.reshape((2, CORES) + own.shape)
    smem = pl.BlockSpec(memory_space=pltpu.SMEM)
    vmem = pl.BlockSpec(memory_space=pltpu.VMEM)
    wide = (src_count, LANES)
    targets, scale, lanes_t, lanes_s = pl.pallas_call(
        target_kernel,
        in_specs=[smem] + [vmem] * 3,
        out_specs=[vmem] * 4,
        out_shape=[
            jax.ShapeDtypeStruct((source.shape[0], tgt_count), jnp.bfloat16),
            jax.ShapeDtypeStruct((1, tgt_count), jnp.float32),
            jax.ShapeDtypeStruct(wide, jnp.int32),
            jax.ShapeDtypeStruct((tgt_count, LANES), jnp.int32),
        ],
        compiler_params=pltpu.CompilerParams(vmem_limit_bytes=32 * 1024 * 1024),
        cost_estimate=pl.CostEstimate(flops=1_000_000, bytes_accessed=2**20, transcendentals=256),
    )(starts, halves, src_near.T, tgt_near.T)
    cosines, row, col = pl.pallas_call(
        tile_kernel,
        in_specs=[vmem] * 5,
        out_specs=[vmem] * 3,
        out_shape=[
            jax.ShapeDtypeStruct((src_count, tgt_count), jnp.float32),
            jax.ShapeDtypeStruct((1, src_count), jnp.float32),
            jax.ShapeDtypeStruct((1, tgt_count), jnp.float32),
        ],
        compiler_params=pltpu.CompilerParams(vmem_limit_bytes=32 * 1024 * 1024),
        cost_estimate=pl.CostEstimate(flops=300_000_000, bytes_accessed=2**21, transcendentals=512),
    )(source, targets, scale, lanes_t, lanes_s)

    first = core == 0
    both = lax.all_gather(
        jnp.concatenate([row, col], axis=0), "src", axis=0, axis_index_groups=pairs
    )
    sums = jnp.where(first, both[:, 0], jnp.broadcast_to(jnp.sum(both[:, 1], axis=0), (2, tgt_count)))
    parts = lax.all_to_all(spread(sums, chips), ("src", "tgt"), 0, 0, axis_index_groups=lines)
    averages = jnp.sum(parts, axis=0) / near_count
    both = lax.all_gather(averages, "src", axis=0, axis_index_groups=pairs)
    margin, src_average, tgt_average = pl.pallas_call(
        margin_kernel,
        in_specs=[smem] + [vmem] * 2,
        out_specs=[vmem] * 3,
        out_shape=[
            jax.ShapeDtypeStruct((src_count, tgt_count), jnp.bfloat16),
            jax.ShapeDtypeStruct((1, src_count), jnp.float32),
            jax.ShapeDtypeStruct((1, tgt_count), jnp.float32),
        ],
        compiler_params=pltpu.CompilerParams(vmem_limit_bytes=8 * 1024 * 1024),
        cost_estimate=pl.CostEstimate(flops=200_000, bytes_accessed=2**19, transcendentals=0),
    )(core.astype(jnp.int32).reshape(1), both, cosines)
    return (margin, src_average.reshape(src_count), tgt_average.reshape(tgt_count))


def solution(mesh):
    placed = (P("src", "tgt"), P("tgt", "src"), P("src", None), P("tgt", None))
    return jax.shard_map(
        local,
        mesh=mesh,
        in_specs=placed,
        out_specs=(P("src", "tgt"), P("src"), P("tgt")),
        check_vma=False,
    )
```

```python
import itertools

import jax
import jax.numpy as jnp
from jax import lax
from jax.experimental import pallas as pl
from jax.experimental.pallas import tpu as pltpu
from jax.sharding import PartitionSpec as P

EPSILON = 1e-06
LANES = 128
CORES = 2
MAJOR = (((0,), (0,)), ((), ()))


def spread(values, count):
    return jnp.broadcast_to(values[None], (count,) + values.shape)


def inverse_norms(values):
    wide = values.astype(jnp.float32)
    return lax.rsqrt(jnp.sum(wide * wide, axis=0, keepdims=True) + EPSILON)


def picked(cosines, index):
    total = jnp.zeros(index.shape, jnp.float32)
    for half in range(cosines.shape[1] // LANES):
        block = cosines[:, half * LANES : (half + 1) * LANES]
        found = jnp.take_along_axis(block, index & (LANES - 1), axis=1)
        total = total + jnp.where(index >> 7 == half, found, 0.0)
    return jnp.sum(total.T, axis=0, keepdims=True)


def lanes_of(near, start):
    count, rows = near.shape
    fill = jnp.full((LANES - count, rows), -1, jnp.int32)
    return jnp.concatenate([near - start, fill], axis=0).T


def target_kernel(start_ref, t_ref, near_t_ref, near_s_ref, ordered_ref, scale_ref, lanes_t_ref, lanes_s_ref):
    layer = start_ref[2]
    order = itertools.product(range(t_ref.shape[2]), range(2), range(t_ref.shape[0]))
    pieces = [t_ref[c, lax.rem(layer + h, 2), p] for p, h, c in order]
    targets = jnp.concatenate(pieces, axis=0)
    ordered_ref[...] = targets
    scale_ref[...] = inverse_norms(targets)
    lanes_t_ref[...] = lanes_of(near_t_ref[...], start_ref[0])
    lanes_s_ref[...] = lanes_of(near_s_ref[...], start_ref[1])


def tile_kernel(s_ref, t_ref, scale_ref, lanes_t_ref, lanes_s_ref, cos_ref, row_ref, col_ref):
    sources = s_ref[...]
    targets = t_ref[...]
    s_scale = inverse_norms(sources)

    column = jnp.broadcast_to(s_scale, (8, s_scale.shape[1])).T[:, :1]
    products = lax.dot_general(sources, targets, MAJOR, preferred_element_type=jnp.float32)
    cosines = products * column * scale_ref[...]
    cos_ref[...] = cosines
    row_ref[...] = picked(cosines, lanes_t_ref[...])
    col_ref[...] = picked(cosines.T, lanes_s_ref[...])


def margin_kernel(core_ref, both_ref, cos_ref, margin_ref, src_ref, tgt_ref):
    src_average = both_ref[0, pl.ds(core_ref[0], 1)]
    tgt_average = both_ref[1, :1]
    src_ref[...] = src_average
    tgt_ref[...] = tgt_average
    rows = src_average.shape[1]
    column = jnp.broadcast_to(src_average, (8, rows)).T[:, :1]
    margin_ref[...] = (cos_ref[...] / ((column + tgt_average) / 2.0)).astype(jnp.bfloat16)


def local(src_embed, tgt_embed, src_near, tgt_near):
    src_index = lax.axis_index("src")
    tgt_index = lax.axis_index("tgt")
    core = src_index % CORES
    src_size = lax.axis_size("src")
    tgt_size = lax.axis_size("tgt")
    chips = src_size // CORES
    src_count, near_count = src_near.shape
    tgt_count = tgt_near.shape[0]
    pairs = [[q * CORES + c for c in range(CORES)] for q in range(chips)]
    line = tgt_size // 2
    layer = tgt_index // line
    partners = [(k, k ^ line) for k in range(tgt_size)]
    lines_y = [[h * line + k for k in range(line)] for h in range(2)]

    half = src_size // 2
    blocks = [[k * half + q * CORES + c for q in range(chips // 2)] for k in range(2) for c in range(CORES)]
    far_pairs = [[k, k + half] for k in range(half)]

    def index_of(s, t):
        return s * tgt_size + t

    lines = [[index_of(q * CORES, t) for t in range(tgt_size)] for q in range(chips)]
    lines += [[index_of(q * CORES + 1, t) for q in range(chips)] for t in range(tgt_size)]

    starts = jnp.stack([tgt_index * tgt_count, src_index * src_count, layer]).astype(jnp.int32)
    mine = src_embed.T
    partner = lax.ppermute(mine, "tgt", partners)
    copies = len(blocks[0])
    own = lax.cond(
        src_index + tgt_index < src_size + tgt_size,
        lambda part: lax.all_to_all(spread(part, copies), "src", 0, 0, axis_index_groups=blocks),
        lambda part: lax.all_gather(part, "src", axis=0, axis_index_groups=blocks),
        tgt_embed.T,
    )
    own, mine, partner = lax.optimization_barrier((own, mine, partner))
    operand = spread(jnp.stack([mine, partner]), line)
    source = lax.all_to_all(operand, "tgt", 0, 0, axis_index_groups=lines_y)
    source = source.reshape(-1, src_count)
    halves = lax.all_gather(own, "src", axis=0, axis_index_groups=far_pairs)
    halves = lax.all_gather(halves, "src", axis=0, axis_index_groups=pairs)
    smem = pl.BlockSpec(memory_space=pltpu.SMEM)
    vmem = pl.BlockSpec(memory_space=pltpu.VMEM)
    wide = (src_count, LANES)
    targets, scale, lanes_t, lanes_s = pl.pallas_call(
        target_kernel,
        in_specs=[smem] + [vmem] * 3,
        out_specs=[vmem] * 4,
        out_shape=[
            jax.ShapeDtypeStruct((source.shape[0], tgt_count), jnp.bfloat16),
            jax.ShapeDtypeStruct((1, tgt_count), jnp.float32),
            jax.ShapeDtypeStruct(wide, jnp.int32),
            jax.ShapeDtypeStruct((tgt_count, LANES), jnp.int32),
        ],
        compiler_params=pltpu.CompilerParams(vmem_limit_bytes=32 * 1024 * 1024),
        cost_estimate=pl.CostEstimate(flops=1_000_000, bytes_accessed=2**20, transcendentals=256),
    )(starts, halves, src_near.T, tgt_near.T)
    cosines, row, col = pl.pallas_call(
        tile_kernel,
        in_specs=[vmem] * 5,
        out_specs=[vmem] * 3,
        out_shape=[
            jax.ShapeDtypeStruct((src_count, tgt_count), jnp.float32),
            jax.ShapeDtypeStruct((1, src_count), jnp.float32),
            jax.ShapeDtypeStruct((1, tgt_count), jnp.float32),
        ],
        compiler_params=pltpu.CompilerParams(vmem_limit_bytes=32 * 1024 * 1024),
        cost_estimate=pl.CostEstimate(flops=300_000_000, bytes_accessed=2**21, transcendentals=512),
    )(source, targets, scale, lanes_t, lanes_s)

    first = core == 0
    both = lax.all_gather(
        jnp.concatenate([row, col], axis=0), "src", axis=0, axis_index_groups=pairs
    )
    sums = jnp.where(first, both[:, 0], jnp.broadcast_to(jnp.sum(both[:, 1], axis=0), (2, tgt_count)))
    parts = lax.all_to_all(spread(sums, chips), ("src", "tgt"), 0, 0, axis_index_groups=lines)
    averages = jnp.sum(parts, axis=0) / near_count
    both = lax.all_gather(averages, "src", axis=0, axis_index_groups=pairs)
    margin, src_average, tgt_average = pl.pallas_call(
        margin_kernel,
        in_specs=[smem] + [vmem] * 2,
        out_specs=[vmem] * 3,
        out_shape=[
            jax.ShapeDtypeStruct((src_count, tgt_count), jnp.bfloat16),
            jax.ShapeDtypeStruct((1, src_count), jnp.float32),
            jax.ShapeDtypeStruct((1, tgt_count), jnp.float32),
        ],
        compiler_params=pltpu.CompilerParams(vmem_limit_bytes=8 * 1024 * 1024),
        cost_estimate=pl.CostEstimate(flops=200_000, bytes_accessed=2**19, transcendentals=0),
    )(core.astype(jnp.int32).reshape(1), both, cosines)
    return (margin, src_average.reshape(src_count), tgt_average.reshape(tgt_count))


def solution(mesh):
    placed = (P("src", "tgt"), P("tgt", "src"), P("src", None), P("tgt", None))
    return jax.shard_map(
        local,
        mesh=mesh,
        in_specs=placed,
        out_specs=(P("src", "tgt"), P("src"), P("tgt")),
        check_vma=False,
    )
```

```python
import itertools

import jax
import jax.numpy as jnp
from jax import lax
from jax.experimental import pallas as pl
from jax.experimental.pallas import tpu as pltpu
from jax.sharding import PartitionSpec as P

EPSILON = 1e-06
LANES = 128
CORES = 2
MAJOR = (((0,), (0,)), ((), ()))


def spread(values, count):
    return jnp.broadcast_to(values[None], (count,) + values.shape)


def inverse_norms(values):
    wide = values.astype(jnp.float32)
    return lax.rsqrt(jnp.sum(wide * wide, axis=0, keepdims=True) + EPSILON)


def picked(cosines, index):
    total = jnp.zeros(index.shape, jnp.float32)
    for half in range(cosines.shape[1] // LANES):
        block = cosines[:, half * LANES : (half + 1) * LANES]
        found = jnp.take_along_axis(block, index & (LANES - 1), axis=1)
        total = total + jnp.where(index >> 7 == half, found, 0.0)
    return jnp.sum(total.T, axis=0, keepdims=True)


def lanes_of(near, start):
    count, rows = near.shape
    fill = jnp.full((LANES - count, rows), -1, jnp.int32)
    return jnp.concatenate([near - start, fill], axis=0).T


def target_kernel(start_ref, t_ref, near_t_ref, near_s_ref, ordered_ref, scale_ref, lanes_t_ref, lanes_s_ref):
    layer = start_ref[2]
    order = itertools.product(range(t_ref.shape[2]), range(2), range(t_ref.shape[0]))
    pieces = [t_ref[c, lax.rem(layer + h, 2), p] for p, h, c in order]
    targets = jnp.concatenate(pieces, axis=0)
    ordered_ref[...] = targets
    scale_ref[...] = inverse_norms(targets)
    lanes_t_ref[...] = lanes_of(near_t_ref[...], start_ref[0])
    lanes_s_ref[...] = lanes_of(near_s_ref[...], start_ref[1])


def tile_kernel(s_ref, t_ref, scale_ref, lanes_t_ref, lanes_s_ref, cos_ref, row_ref, col_ref):
    sources = s_ref[...]
    targets = t_ref[...]
    s_scale = inverse_norms(sources)

    column = jnp.broadcast_to(s_scale, (8, s_scale.shape[1])).T[:, :1]
    products = lax.dot_general(sources, targets, MAJOR, preferred_element_type=jnp.float32)
    cosines = products * column * scale_ref[...]
    cos_ref[...] = cosines
    row_ref[...] = picked(cosines, lanes_t_ref[...])
    col_ref[...] = picked(cosines.T, lanes_s_ref[...])


def margin_kernel(core_ref, both_ref, cos_ref, margin_ref, src_ref, tgt_ref):
    src_average = both_ref[1, pl.ds(core_ref[0], 1)]
    tgt_average = both_ref[0, :1]
    src_ref[...] = src_average
    tgt_ref[...] = tgt_average
    rows = src_average.shape[1]
    column = jnp.broadcast_to(src_average, (8, rows)).T[:, :1]
    margin_ref[...] = (cos_ref[...] / ((column + tgt_average) / 2.0)).astype(jnp.bfloat16)


def local(src_embed, tgt_embed, src_near, tgt_near):
    src_index = lax.axis_index("src")
    tgt_index = lax.axis_index("tgt")
    core = src_index % CORES
    src_size = lax.axis_size("src")
    tgt_size = lax.axis_size("tgt")
    chips = src_size // CORES
    src_count, near_count = src_near.shape
    tgt_count = tgt_near.shape[0]
    pairs = [[q * CORES + c for c in range(CORES)] for q in range(chips)]
    line = tgt_size // 2
    layer = tgt_index // line
    partners = [(k, k ^ line) for k in range(tgt_size)]
    lines_y = [[h * line + k for k in range(line)] for h in range(2)]

    half = src_size // 2
    blocks = [[k * half + q * CORES + c for q in range(chips // 2)] for k in range(2) for c in range(CORES)]
    far_pairs = [[k, k + half] for k in range(half)]

    def index_of(s, t):
        return s * tgt_size + t

    lines = [[index_of(q * CORES + 1, t) for t in range(tgt_size)] for q in range(chips)]
    lines += [[index_of(q * CORES, t) for q in range(chips)] for t in range(tgt_size)]

    starts = jnp.stack([tgt_index * tgt_count, src_index * src_count, layer]).astype(jnp.int32)
    mine = src_embed.T
    partner = lax.ppermute(mine, "tgt", partners)
    copies = len(blocks[0])
    own = lax.cond(
        src_index + tgt_index < src_size + tgt_size,
        lambda part: lax.all_to_all(spread(part, copies), "src", 0, 0, axis_index_groups=blocks),
        lambda part: lax.all_gather(part, "src", axis=0, axis_index_groups=blocks),
        tgt_embed.T,
    )
    own, mine, partner = lax.optimization_barrier((own, mine, partner))
    operand = spread(jnp.stack([mine, partner]), line)
    source = lax.all_to_all(operand, "tgt", 0, 0, axis_index_groups=lines_y)
    source = source.reshape(-1, src_count)
    halves = lax.all_gather(own, "src", axis=0, axis_index_groups=far_pairs)
    halves = lax.all_gather(halves, "src", axis=0, axis_index_groups=pairs)
    smem = pl.BlockSpec(memory_space=pltpu.SMEM)
    vmem = pl.BlockSpec(memory_space=pltpu.VMEM)
    wide = (src_count, LANES)
    targets, scale, lanes_t, lanes_s = pl.pallas_call(
        target_kernel,
        in_specs=[smem] + [vmem] * 3,
        out_specs=[vmem] * 4,
        out_shape=[
            jax.ShapeDtypeStruct((source.shape[0], tgt_count), jnp.bfloat16),
            jax.ShapeDtypeStruct((1, tgt_count), jnp.float32),
            jax.ShapeDtypeStruct(wide, jnp.int32),
            jax.ShapeDtypeStruct((tgt_count, LANES), jnp.int32),
        ],
        compiler_params=pltpu.CompilerParams(vmem_limit_bytes=32 * 1024 * 1024),
        cost_estimate=pl.CostEstimate(flops=1_000_000, bytes_accessed=2**20, transcendentals=256),
    )(starts, halves, src_near.T, tgt_near.T)
    cosines, row, col = pl.pallas_call(
        tile_kernel,
        in_specs=[vmem] * 5,
        out_specs=[vmem] * 3,
        out_shape=[
            jax.ShapeDtypeStruct((src_count, tgt_count), jnp.float32),
            jax.ShapeDtypeStruct((1, src_count), jnp.float32),
            jax.ShapeDtypeStruct((1, tgt_count), jnp.float32),
        ],
        compiler_params=pltpu.CompilerParams(vmem_limit_bytes=32 * 1024 * 1024),
        cost_estimate=pl.CostEstimate(flops=300_000_000, bytes_accessed=2**21, transcendentals=512),
    )(source, targets, scale, lanes_t, lanes_s)

    by_rows = core == 1
    both = lax.all_gather(
        jnp.concatenate([row, col], axis=0), "src", axis=0, axis_index_groups=pairs
    )
    sums = jnp.where(by_rows, both[:, 0], jnp.broadcast_to(jnp.sum(both[:, 1], axis=0), (2, tgt_count)))
    parts = lax.all_to_all(spread(sums, chips), ("src", "tgt"), 0, 0, axis_index_groups=lines)
    averages = jnp.sum(parts, axis=0) / near_count
    both = lax.all_gather(averages, "src", axis=0, axis_index_groups=pairs)
    margin, src_average, tgt_average = pl.pallas_call(
        margin_kernel,
        in_specs=[smem] + [vmem] * 2,
        out_specs=[vmem] * 3,
        out_shape=[
            jax.ShapeDtypeStruct((src_count, tgt_count), jnp.bfloat16),
            jax.ShapeDtypeStruct((1, src_count), jnp.float32),
            jax.ShapeDtypeStruct((1, tgt_count), jnp.float32),
        ],
        compiler_params=pltpu.CompilerParams(vmem_limit_bytes=8 * 1024 * 1024),
        cost_estimate=pl.CostEstimate(flops=200_000, bytes_accessed=2**19, transcendentals=0),
    )(core.astype(jnp.int32).reshape(1), both, cosines)
    return (margin, src_average.reshape(src_count), tgt_average.reshape(tgt_count))


def solution(mesh):
    placed = (P("src", "tgt"), P("tgt", "src"), P("src", None), P("tgt", None))
    return jax.shard_map(
        local,
        mesh=mesh,
        in_specs=placed,
        out_specs=(P("src", "tgt"), P("src"), P("tgt")),
        check_vma=False,
    )
```

```python
import functools
import itertools

import jax
import jax.numpy as jnp
from jax import lax
from jax.experimental import pallas as pl
from jax.experimental.pallas import tpu as pltpu
from jax.sharding import PartitionSpec as P

EPSILON = 1e-06
LANES = 128
CORES = 2
MAJOR = (((0,), (0,)), ((), ()))


def spread(values, count):
    return jnp.broadcast_to(values[None], (count,) + values.shape)


def inverse_norms(values):
    wide = values.astype(jnp.float32)
    return lax.rsqrt(jnp.sum(wide * wide, axis=0, keepdims=True) + EPSILON)


def picked(cosines, index, first, count):
    total = jnp.zeros(index.shape, jnp.float32)
    for half in range(cosines.shape[1] // LANES):
        block = cosines[:, half * LANES : (half + 1) * LANES]
        found = jnp.take_along_axis(block, index & (LANES - 1), axis=1)
        total = jnp.where(index >> 7 == half, found, total)
    return jnp.sum(total.T[first : first + count], axis=0, keepdims=True)


def lanes_of(near_t, near_s):
    fill = jnp.full((LANES - near_t.shape[0] - near_s.shape[0], near_t.shape[1]), -1, jnp.int32)
    return jnp.concatenate([near_t, near_s, fill], axis=0).T


def target_kernel(start_ref, t_ref, near_t_ref, near_s_ref, ordered_ref, scale_ref, lanes_ref):
    layer = start_ref[2]
    order = itertools.product(range(t_ref.shape[2]), range(2), range(t_ref.shape[0]))
    pieces = [t_ref[c, lax.rem(layer + h, 2), p] for p, h, c in order]
    targets = jnp.concatenate(pieces, axis=0)
    ordered_ref[...] = targets
    scale_ref[...] = inverse_norms(targets)
    lanes_ref[...] = lanes_of(near_t_ref[...] - start_ref[0], near_s_ref[...] - start_ref[1])


def tile_kernel(near_count, s_ref, t_ref, scale_ref, lanes_ref, cos_ref, row_ref, col_ref):
    sources = s_ref[...]
    targets = t_ref[...]
    s_scale = inverse_norms(sources)

    column = jnp.broadcast_to(s_scale, (8, s_scale.shape[1])).T[:, :1]
    products = lax.dot_general(sources, targets, MAJOR, preferred_element_type=jnp.float32)
    cosines = products * column * scale_ref[...]
    cos_ref[...] = cosines
    lanes = lanes_ref[...]
    row_ref[...] = picked(cosines, lanes, 0, near_count)
    col_ref[...] = picked(cosines.T, lanes, near_count, near_count)


def margin_kernel(core_ref, both_ref, cos_ref, margin_ref, src_ref, tgt_ref):
    src_average = both_ref[1, pl.ds(core_ref[0], 1)]
    tgt_average = both_ref[0, :1]
    src_ref[...] = src_average
    tgt_ref[...] = tgt_average
    rows = src_average.shape[1]
    column = jnp.broadcast_to(src_average, (8, rows)).T[:, :1]
    margin_ref[...] = (cos_ref[...] / ((column + tgt_average) / 2.0)).astype(jnp.bfloat16)


def local(src_embed, tgt_embed, src_near, tgt_near):
    src_index = lax.axis_index("src")
    tgt_index = lax.axis_index("tgt")
    core = src_index % CORES
    src_size = lax.axis_size("src")
    tgt_size = lax.axis_size("tgt")
    chips = src_size // CORES
    src_count, near_count = src_near.shape
    tgt_count = tgt_near.shape[0]
    pairs = [[q * CORES + c for c in range(CORES)] for q in range(chips)]
    line = tgt_size // 2
    layer = tgt_index // line
    partners = [(k, k ^ line) for k in range(tgt_size)]
    lines_y = [[h * line + k for k in range(line)] for h in range(2)]

    half = src_size // 2
    blocks = [[k * half + q * CORES + c for q in range(chips // 2)] for k in range(2) for c in range(CORES)]
    far_pairs = [[k, k + half] for k in range(half)]

    def index_of(s, t):
        return s * tgt_size + t

    lines = [[index_of(q * CORES + 1, t) for t in range(tgt_size)] for q in range(chips)]
    lines += [[index_of(q * CORES, t) for q in range(chips)] for t in range(tgt_size)]

    starts = jnp.stack([tgt_index * tgt_count, src_index * src_count, layer]).astype(jnp.int32)
    mine = src_embed.T
    partner = lax.ppermute(mine, "tgt", partners)
    copies = len(blocks[0])
    own = lax.cond(
        src_index + tgt_index < src_size + tgt_size,
        lambda part: lax.all_to_all(spread(part, copies), "src", 0, 0, axis_index_groups=blocks),
        lambda part: lax.all_gather(part, "src", axis=0, axis_index_groups=blocks),
        tgt_embed.T,
    )
    own, mine, partner = lax.optimization_barrier((own, mine, partner))
    operand = spread(jnp.stack([mine, partner]), line)
    source = lax.all_to_all(operand, "tgt", 0, 0, axis_index_groups=lines_y)
    source = source.reshape(-1, src_count)
    halves = lax.all_gather(own, "src", axis=0, axis_index_groups=far_pairs)
    halves = lax.all_gather(halves, "src", axis=0, axis_index_groups=pairs)
    smem = pl.BlockSpec(memory_space=pltpu.SMEM)
    vmem = pl.BlockSpec(memory_space=pltpu.VMEM)
    wide = (src_count, LANES)
    targets, scale, lanes = pl.pallas_call(
        target_kernel,
        in_specs=[smem] + [vmem] * 3,
        out_specs=[vmem] * 3,
        out_shape=[
            jax.ShapeDtypeStruct((source.shape[0], tgt_count), jnp.bfloat16),
            jax.ShapeDtypeStruct((1, tgt_count), jnp.float32),
            jax.ShapeDtypeStruct(wide, jnp.int32),
        ],
        compiler_params=pltpu.CompilerParams(vmem_limit_bytes=32 * 1024 * 1024),
        cost_estimate=pl.CostEstimate(flops=1_000_000, bytes_accessed=2**20, transcendentals=256),
    )(starts, halves, src_near.T, tgt_near.T)
    cosines, row, col = pl.pallas_call(
        functools.partial(tile_kernel, near_count),
        in_specs=[vmem] * 4,
        out_specs=[vmem] * 3,
        out_shape=[
            jax.ShapeDtypeStruct((src_count, tgt_count), jnp.float32),
            jax.ShapeDtypeStruct((1, src_count), jnp.float32),
            jax.ShapeDtypeStruct((1, tgt_count), jnp.float32),
        ],
        compiler_params=pltpu.CompilerParams(vmem_limit_bytes=32 * 1024 * 1024),
        cost_estimate=pl.CostEstimate(flops=300_000_000, bytes_accessed=2**21, transcendentals=512),
    )(source, targets, scale, lanes)

    by_rows = core == 1
    both = lax.all_gather(
        jnp.concatenate([row, col], axis=0), "src", axis=0, axis_index_groups=pairs
    )
    sums = jnp.where(by_rows, both[:, 0], jnp.broadcast_to(jnp.sum(both[:, 1], axis=0), (2, tgt_count)))
    parts = lax.all_to_all(spread(sums, chips), ("src", "tgt"), 0, 0, axis_index_groups=lines)
    averages = jnp.sum(parts, axis=0) / near_count
    both = lax.all_gather(averages, "src", axis=0, axis_index_groups=pairs)
    margin, src_average, tgt_average = pl.pallas_call(
        margin_kernel,
        in_specs=[smem] + [vmem] * 2,
        out_specs=[vmem] * 3,
        out_shape=[
            jax.ShapeDtypeStruct((src_count, tgt_count), jnp.bfloat16),
            jax.ShapeDtypeStruct((1, src_count), jnp.float32),
            jax.ShapeDtypeStruct((1, tgt_count), jnp.float32),
        ],
        compiler_params=pltpu.CompilerParams(vmem_limit_bytes=8 * 1024 * 1024),
        cost_estimate=pl.CostEstimate(flops=200_000, bytes_accessed=2**19, transcendentals=0),
    )(core.astype(jnp.int32).reshape(1), both, cosines)
    return (margin, src_average.reshape(src_count), tgt_average.reshape(tgt_count))


def solution(mesh):
    placed = (P("src", "tgt"), P("tgt", "src"), P("src", None), P("tgt", None))
    return jax.shard_map(
        local,
        mesh=mesh,
        in_specs=placed,
        out_specs=(P("src", "tgt"), P("src"), P("tgt")),
        check_vma=False,
    )
```

```python
import functools
import itertools

import jax
import jax.numpy as jnp
from jax import lax
from jax.experimental import pallas as pl
from jax.experimental.pallas import tpu as pltpu
from jax.sharding import PartitionSpec as P

EPSILON = 1e-06
LANES = 128
CORES = 2
MAJOR = (((0,), (0,)), ((), ()))


def spread(values, count):
    return jnp.broadcast_to(values[None], (count,) + values.shape)


def inverse_norms(values):
    wide = values.astype(jnp.float32)
    return lax.rsqrt(jnp.sum(wide * wide, axis=0, keepdims=True) + EPSILON)


def picked(cosines, index, first, count):
    total = jnp.zeros(index.shape, jnp.float32)
    for half in range(cosines.shape[1] // LANES):
        block = cosines[:, half * LANES : (half + 1) * LANES]
        found = jnp.take_along_axis(block, index & (LANES - 1), axis=1)
        total = jnp.where(index >> 7 == half, found, total)
    return jnp.sum(total.T[first : first + count], axis=0, keepdims=True)


def lanes_of(near_t, near_s):
    fill = jnp.full((LANES - near_t.shape[0] - near_s.shape[0], near_t.shape[1]), -1, jnp.int32)
    return jnp.concatenate([near_t, near_s, fill], axis=0).T


def target_kernel(start_ref, t_ref, near_t_ref, near_s_ref, ordered_ref, scale_ref, lanes_ref):
    layer = start_ref[2]
    order = itertools.product(range(t_ref.shape[2]), range(2), range(t_ref.shape[0]))
    pieces = [t_ref[c, lax.rem(layer + h, 2), p] for p, h, c in order]
    targets = jnp.concatenate(pieces, axis=0)
    ordered_ref[...] = targets
    scale_ref[...] = inverse_norms(targets)
    lanes_ref[...] = lanes_of(near_t_ref[...] - start_ref[0], near_s_ref[...] - start_ref[1])


def tile_kernel(near_count, s_ref, t_ref, scale_ref, lanes_ref, cos_ref, sums_ref):
    sources = s_ref[...]
    targets = t_ref[...]
    s_scale = inverse_norms(sources)

    column = jnp.broadcast_to(s_scale, (8, s_scale.shape[1])).T[:, :1]
    products = lax.dot_general(sources, targets, MAJOR, preferred_element_type=jnp.float32)
    cosines = products * column * scale_ref[...]
    cos_ref[...] = cosines
    lanes = lanes_ref[...]
    by_row = picked(cosines, lanes, 0, near_count)
    by_column = picked(cosines.T, lanes, near_count, near_count)
    sums_ref[...] = jnp.concatenate([by_row, by_column], axis=0)


def margin_kernel(core_ref, both_ref, cos_ref, margin_ref, src_ref, tgt_ref, staged, sems):
    src_average = both_ref[1, pl.ds(core_ref[0], 1)]
    tgt_average = both_ref[0, :1]
    src_ref[...] = src_average
    tgt_ref[...] = tgt_average
    rows = src_average.shape[1]
    column = jnp.broadcast_to(src_average, (8, rows)).T[:, :1]
    half = rows // 2
    copies = []
    for k in range(2):
        part = slice(k * half, (k + 1) * half)
        staged[part] = (cos_ref[part] / ((column[part] + tgt_average) / 2.0)).astype(jnp.bfloat16)
        copies.append(pltpu.make_async_copy(staged.at[part], margin_ref.at[part], sems.at[k]))
        copies[k].start()
    for copy in copies:
        copy.wait()


def local(src_embed, tgt_embed, src_near, tgt_near):
    src_index = lax.axis_index("src")
    tgt_index = lax.axis_index("tgt")
    core = src_index % CORES
    src_size = lax.axis_size("src")
    tgt_size = lax.axis_size("tgt")
    chips = src_size // CORES
    src_count, near_count = src_near.shape
    tgt_count = tgt_near.shape[0]
    pairs = [[q * CORES + c for c in range(CORES)] for q in range(chips)]
    line = tgt_size // 2
    layer = tgt_index // line
    partners = [(k, k ^ line) for k in range(tgt_size)]
    lines_y = [[h * line + k for k in range(line)] for h in range(2)]

    half = src_size // 2
    blocks = [[k * half + q * CORES + c for q in range(chips // 2)] for k in range(2) for c in range(CORES)]
    far_pairs = [[k, k + half] for k in range(half)]

    def index_of(s, t):
        return s * tgt_size + t

    lines = [[index_of(q * CORES + 1, t) for t in range(tgt_size)] for q in range(chips)]
    lines += [[index_of(q * CORES, t) for q in range(chips)] for t in range(tgt_size)]

    starts = jnp.stack([tgt_index * tgt_count, src_index * src_count, layer]).astype(jnp.int32)
    mine = src_embed.T
    partner = lax.ppermute(mine, "tgt", partners)
    copies = len(blocks[0])
    own = lax.cond(
        src_index + tgt_index < src_size + tgt_size,
        lambda part: lax.all_to_all(spread(part, copies), "src", 0, 0, axis_index_groups=blocks),
        lambda part: lax.all_gather(part, "src", axis=0, axis_index_groups=blocks),
        tgt_embed.T,
    )
    own, mine, partner = lax.optimization_barrier((own, mine, partner))
    operand = spread(jnp.stack([mine, partner]), line)
    source = lax.all_to_all(operand, "tgt", 0, 0, axis_index_groups=lines_y)
    source = source.reshape(-1, src_count)
    halves = lax.all_gather(own, "src", axis=0, axis_index_groups=far_pairs)
    halves = lax.all_gather(halves, "src", axis=0, axis_index_groups=pairs)
    smem = pl.BlockSpec(memory_space=pltpu.SMEM)
    vmem = pl.BlockSpec(memory_space=pltpu.VMEM)
    wide = (src_count, LANES)
    targets, scale, lanes = pl.pallas_call(
        target_kernel,
        in_specs=[smem] + [vmem] * 3,
        out_specs=[vmem] * 3,
        out_shape=[
            jax.ShapeDtypeStruct((source.shape[0], tgt_count), jnp.bfloat16),
            jax.ShapeDtypeStruct((1, tgt_count), jnp.float32),
            jax.ShapeDtypeStruct(wide, jnp.int32),
        ],
        compiler_params=pltpu.CompilerParams(vmem_limit_bytes=32 * 1024 * 1024),
        cost_estimate=pl.CostEstimate(flops=1_000_000, bytes_accessed=2**20, transcendentals=256),
    )(starts, halves, src_near.T, tgt_near.T)
    cosines, sums = pl.pallas_call(
        functools.partial(tile_kernel, near_count),
        in_specs=[vmem] * 4,
        out_specs=[vmem] * 2,
        out_shape=[
            jax.ShapeDtypeStruct((src_count, tgt_count), jnp.float32),
            jax.ShapeDtypeStruct((2, src_count), jnp.float32),
        ],
        compiler_params=pltpu.CompilerParams(vmem_limit_bytes=32 * 1024 * 1024),
        cost_estimate=pl.CostEstimate(flops=300_000_000, bytes_accessed=2**21, transcendentals=512),
    )(source, targets, scale, lanes)

    by_rows = core == 1
    both = lax.all_gather(sums, "src", axis=0, axis_index_groups=pairs)
    sums = jnp.where(by_rows, both[:, 0], jnp.broadcast_to(jnp.sum(both[:, 1], axis=0), (2, tgt_count)))
    parts = lax.all_to_all(spread(sums, chips), ("src", "tgt"), 0, 0, axis_index_groups=lines)
    averages = jnp.sum(parts, axis=0) / near_count
    both = lax.all_gather(averages, "src", axis=0, axis_index_groups=pairs)
    margin, src_average, tgt_average = pl.pallas_call(
        margin_kernel,
        in_specs=[smem] + [vmem] * 2,
        out_specs=[pl.BlockSpec(memory_space=pl.ANY)] + [vmem] * 2,
        out_shape=[
            jax.ShapeDtypeStruct((src_count, tgt_count), jnp.bfloat16),
            jax.ShapeDtypeStruct((1, src_count), jnp.float32),
            jax.ShapeDtypeStruct((1, tgt_count), jnp.float32),
        ],
        scratch_shapes=[
            pltpu.VMEM((src_count, tgt_count), jnp.bfloat16),
            pltpu.SemaphoreType.DMA((2,)),
        ],
        compiler_params=pltpu.CompilerParams(vmem_limit_bytes=8 * 1024 * 1024),
        cost_estimate=pl.CostEstimate(flops=200_000, bytes_accessed=2**19, transcendentals=0),
    )(core.astype(jnp.int32).reshape(1), both, cosines)
    return (margin, src_average.reshape(src_count), tgt_average.reshape(tgt_count))


def solution(mesh):
    placed = (P("src", "tgt"), P("tgt", "src"), P("src", None), P("tgt", None))
    return jax.shard_map(
        local,
        mesh=mesh,
        in_specs=placed,
        out_specs=(P("src", "tgt"), P("src"), P("tgt")),
        check_vma=False,
    )
```

```python
import functools
import itertools

import jax
import jax.numpy as jnp
from jax import lax
from jax.experimental import pallas as pl
from jax.experimental.pallas import tpu as pltpu
from jax.sharding import PartitionSpec as P

EPSILON = 1e-06
LANES = 128
CORES = 2
MAJOR = (((0,), (0,)), ((), ()))


def spread(values, count):
    return jnp.broadcast_to(values[None], (count,) + values.shape)


def inverse_norms(values):
    wide = values.astype(jnp.float32)
    return lax.rsqrt(jnp.sum(wide * wide, axis=0, keepdims=True) + EPSILON)


def picked(cosines, index, first, count):
    total = jnp.zeros(index.shape, jnp.float32)
    for half in range(cosines.shape[1] // LANES):
        block = cosines[:, half * LANES : (half + 1) * LANES]
        found = jnp.take_along_axis(block, index & (LANES - 1), axis=1)
        total = jnp.where(index >> 7 == half, found, total)
    return jnp.sum(total.T[first : first + count], axis=0, keepdims=True)


def lanes_of(near_t, near_s):
    fill = jnp.full((LANES - near_t.shape[0] - near_s.shape[0], near_t.shape[1]), -1, jnp.int32)
    return jnp.concatenate([near_t, near_s, fill], axis=0).T


def target_kernel(start_ref, t_ref, near_t_ref, near_s_ref, ordered_ref, scale_ref, lanes_ref):
    layer = start_ref[2]
    order = itertools.product(range(t_ref.shape[2]), range(2), range(t_ref.shape[0]))
    pieces = [t_ref[c, lax.rem(layer + h, 2), p] for p, h, c in order]
    targets = jnp.concatenate(pieces, axis=0)
    ordered_ref[...] = targets
    scale_ref[...] = inverse_norms(targets)
    lanes_ref[...] = lanes_of(near_t_ref[...] - start_ref[0], near_s_ref[...] - start_ref[1])


def tile_kernel(near_count, s_ref, t_ref, scale_ref, lanes_ref, cos_ref, sums_ref):
    sources = s_ref[...]
    targets = t_ref[...]
    s_scale = inverse_norms(sources)

    column = jnp.broadcast_to(s_scale, (8, s_scale.shape[1])).T[:, :1]
    products = lax.dot_general(sources, targets, MAJOR, preferred_element_type=jnp.float32)
    cosines = products * column * scale_ref[...]
    cos_ref[...] = cosines
    lanes = lanes_ref[...]
    by_row = picked(cosines, lanes, 0, near_count)
    by_column = picked(cosines.T, lanes, near_count, near_count)
    sums_ref[...] = jnp.concatenate([by_row, by_column], axis=0)


def margin_kernel(core_ref, both_ref, cos_ref, margin_ref, src_ref, tgt_ref):
    src_average = both_ref[1, pl.ds(core_ref[0], 1)]
    tgt_average = both_ref[0, :1]
    src_ref[...] = src_average
    tgt_ref[...] = tgt_average
    rows = src_average.shape[1]
    column = jnp.broadcast_to(src_average, (8, rows)).T[:, :1]
    margin_ref[...] = (cos_ref[...] / ((column + tgt_average) / 2.0)).astype(jnp.bfloat16)


def local(src_embed, tgt_embed, src_near, tgt_near):
    src_index = lax.axis_index("src")
    tgt_index = lax.axis_index("tgt")
    core = src_index % CORES
    src_size = lax.axis_size("src")
    tgt_size = lax.axis_size("tgt")
    chips = src_size // CORES
    src_count, near_count = src_near.shape
    tgt_count = tgt_near.shape[0]
    pairs = [[q * CORES + c for c in range(CORES)] for q in range(chips)]
    line = tgt_size // 2
    layer = tgt_index // line
    partners = [(k, k ^ line) for k in range(tgt_size)]
    lines_y = [[h * line + k for k in range(line)] for h in range(2)]

    half = src_size // 2
    blocks = [[k * half + q * CORES + c for q in range(chips // 2)] for k in range(2) for c in range(CORES)]
    far_pairs = [[k, k + half] for k in range(half)]

    def index_of(s, t):
        return s * tgt_size + t

    lines = [[index_of(q * CORES + 1, t) for t in range(tgt_size)] for q in range(chips)]
    lines += [[index_of(q * CORES, t) for q in range(chips)] for t in range(tgt_size)]

    starts = jnp.stack([tgt_index * tgt_count, src_index * src_count, layer]).astype(jnp.int32)
    mine = src_embed.T
    partner = lax.ppermute(mine, "tgt", partners)
    copies = len(blocks[0])
    own = lax.cond(
        src_index + tgt_index < src_size + tgt_size,
        lambda part: lax.all_to_all(spread(part, copies), "src", 0, 0, axis_index_groups=blocks),
        lambda part: lax.all_gather(part, "src", axis=0, axis_index_groups=blocks),
        tgt_embed.T,
    )
    own, mine, partner = lax.optimization_barrier((own, mine, partner))
    operand = spread(jnp.stack([mine, partner]), line)
    source = lax.all_to_all(operand, "tgt", 0, 0, axis_index_groups=lines_y)
    source = source.reshape(-1, src_count)
    halves = lax.all_gather(own, "src", axis=0, axis_index_groups=far_pairs)
    halves = lax.all_gather(halves, "src", axis=0, axis_index_groups=pairs)
    smem = pl.BlockSpec(memory_space=pltpu.SMEM)
    vmem = pl.BlockSpec(memory_space=pltpu.VMEM)
    wide = (src_count, LANES)
    targets, scale, lanes = pl.pallas_call(
        target_kernel,
        in_specs=[smem] + [vmem] * 3,
        out_specs=[vmem] * 3,
        out_shape=[
            jax.ShapeDtypeStruct((source.shape[0], tgt_count), jnp.bfloat16),
            jax.ShapeDtypeStruct((1, tgt_count), jnp.float32),
            jax.ShapeDtypeStruct(wide, jnp.int32),
        ],
        compiler_params=pltpu.CompilerParams(vmem_limit_bytes=32 * 1024 * 1024),
        cost_estimate=pl.CostEstimate(flops=1_000_000, bytes_accessed=2**20, transcendentals=256),
    )(starts, halves, src_near.T, tgt_near.T)
    cosines, sums = pl.pallas_call(
        functools.partial(tile_kernel, near_count),
        in_specs=[vmem] * 4,
        out_specs=[vmem] * 2,
        out_shape=[
            jax.ShapeDtypeStruct((src_count, tgt_count), jnp.float32),
            jax.ShapeDtypeStruct((2, src_count), jnp.float32),
        ],
        compiler_params=pltpu.CompilerParams(vmem_limit_bytes=32 * 1024 * 1024),
        cost_estimate=pl.CostEstimate(flops=300_000_000, bytes_accessed=2**21, transcendentals=512),
    )(source, targets, scale, lanes)

    by_rows = core == 1
    both = lax.all_gather(sums, "src", axis=0, axis_index_groups=pairs)
    sums = jnp.where(by_rows, both[:, 0], jnp.broadcast_to(jnp.sum(both[:, 1], axis=0), (2, tgt_count)))
    parts = lax.all_to_all(spread(sums, chips), ("src", "tgt"), 0, 0, axis_index_groups=lines)
    averages = jnp.sum(parts, axis=0) / near_count
    both = lax.all_gather(averages, "src", axis=0, axis_index_groups=pairs)
    margin, src_average, tgt_average = pl.pallas_call(
        margin_kernel,
        in_specs=[smem] + [vmem] * 2,
        out_specs=[vmem] * 3,
        out_shape=[
            jax.ShapeDtypeStruct((src_count, tgt_count), jnp.bfloat16),
            jax.ShapeDtypeStruct((1, src_count), jnp.float32),
            jax.ShapeDtypeStruct((1, tgt_count), jnp.float32),
        ],
        compiler_params=pltpu.CompilerParams(vmem_limit_bytes=8 * 1024 * 1024),
        cost_estimate=pl.CostEstimate(flops=200_000, bytes_accessed=2**19, transcendentals=0),
    )(core.astype(jnp.int32).reshape(1), both, cosines)
    return (margin, src_average.reshape(src_count), tgt_average.reshape(tgt_count))


def solution(mesh):
    placed = (P("src", "tgt"), P("tgt", "src"), P("src", None), P("tgt", None))
    return jax.shard_map(
        local,
        mesh=mesh,
        in_specs=placed,
        out_specs=(P("src", "tgt"), P("src"), P("tgt")),
        check_vma=False,
    )
```

```python
import functools
import itertools

import jax
import jax.numpy as jnp
from jax import lax
from jax.experimental import pallas as pl
from jax.experimental.pallas import tpu as pltpu
from jax.sharding import PartitionSpec as P

EPSILON = 1e-06
LANES = 128
CORES = 2
MAJOR = (((0,), (0,)), ((), ()))


def spread(values, count):
    return jnp.broadcast_to(values[None], (count,) + values.shape)


def inverse_norms(values):
    wide = values.astype(jnp.float32)
    return lax.rsqrt(jnp.sum(wide * wide, axis=0, keepdims=True) + EPSILON)


def picked(cosines, index, first, count):
    total = jnp.zeros(index.shape, jnp.float32)
    for half in range(cosines.shape[1] // LANES):
        block = cosines[:, half * LANES : (half + 1) * LANES]
        found = jnp.take_along_axis(block, index & (LANES - 1), axis=1)
        total = jnp.where(index >> 7 == half, found, total)
    return jnp.sum(total.T[first : first + count], axis=0, keepdims=True)


def lanes_of(near_t, near_s):
    fill = jnp.full((LANES - near_t.shape[0] - near_s.shape[0], near_t.shape[1]), -1, jnp.int32)
    return jnp.concatenate([near_t, near_s, fill], axis=0).T


def target_kernel(start_ref, t_ref, near_t_ref, near_s_ref, ordered_ref, scale_ref, lanes_ref):
    layer = start_ref[2]
    order = itertools.product(range(t_ref.shape[2]), range(2), range(t_ref.shape[0]))
    pieces = [t_ref[c, lax.rem(layer + h, 2), p] for p, h, c in order]
    targets = jnp.concatenate(pieces, axis=0)
    ordered_ref[...] = targets
    scale_ref[...] = inverse_norms(targets)
    lanes_ref[...] = lanes_of(near_t_ref[...] - start_ref[0], near_s_ref[...] - start_ref[1])


def tile_kernel(near_count, s_ref, t_ref, scale_ref, lanes_ref, cos_ref, sums_ref):
    sources = s_ref[...]
    targets = t_ref[...]
    s_scale = inverse_norms(sources)

    column = jnp.broadcast_to(s_scale, (8, s_scale.shape[1])).T[:, :1]
    products = lax.dot_general(sources, targets, MAJOR, preferred_element_type=jnp.float32)
    cosines = products * column * scale_ref[...]
    cos_ref[...] = cosines
    lanes = lanes_ref[...]
    by_row = picked(cosines, lanes, 0, near_count)
    by_column = picked(cosines.T, lanes, near_count, near_count)
    sums_ref[...] = jnp.concatenate([by_row, by_column], axis=0)


def margin_kernel(core_ref, both_ref, cos_ref, margin_ref, src_ref, tgt_ref):
    src_average = both_ref[1, pl.ds(core_ref[0], 1)]
    tgt_average = both_ref[0, :1]
    src_ref[...] = src_average
    tgt_ref[...] = tgt_average
    rows = src_average.shape[1]
    column = jnp.broadcast_to(src_average, (8, rows)).T[:, :1]
    margin_ref[...] = (cos_ref[...] / ((column + tgt_average) / 2.0)).astype(jnp.bfloat16)


def local(src_embed, tgt_embed, src_near, tgt_near):
    src_index = lax.axis_index("src")
    tgt_index = lax.axis_index("tgt")
    core = src_index % CORES
    src_size = lax.axis_size("src")
    tgt_size = lax.axis_size("tgt")
    chips = src_size // CORES
    src_count, near_count = src_near.shape
    tgt_count = tgt_near.shape[0]
    pairs = [[q * CORES + c for c in range(CORES)] for q in range(chips)]
    line = tgt_size // 2
    layer = tgt_index // line
    partners = [(k, k ^ line) for k in range(tgt_size)]
    lines_y = [[h * line + k for k in range(line)] for h in range(2)]

    half = src_size // 2
    blocks = [[k * half + q * CORES + c for q in range(chips // 2)] for k in range(2) for c in range(CORES)]
    far_pairs = [[k, k + half] for k in range(half)]

    def index_of(s, t):
        return s * tgt_size + t

    lines = [[index_of(q * CORES + 1, t) for t in range(tgt_size)] for q in range(chips)]
    lines += [[index_of(q * CORES, t) for q in range(chips)] for t in range(tgt_size)]

    starts = jnp.stack([tgt_index * tgt_count, src_index * src_count, layer]).astype(jnp.int32)
    mine = src_embed.T
    partner = lax.ppermute(mine, "tgt", partners)
    copies = len(blocks[0])
    own = lax.cond(
        src_index + tgt_index < src_size + tgt_size,
        lambda part: lax.all_to_all(spread(part, copies), "src", 0, 0, axis_index_groups=blocks),
        lambda part: lax.all_gather(part, "src", axis=0, axis_index_groups=blocks),
        tgt_embed.T,
    )
    own, mine, partner = lax.optimization_barrier((own, mine, partner))
    operand = jnp.stack([spread(mine, line), spread(partner, line)], axis=1)
    source = lax.all_to_all(operand, "tgt", 0, 0, axis_index_groups=lines_y)
    source = source.reshape(-1, src_count)
    halves = lax.all_gather(own, "src", axis=0, axis_index_groups=far_pairs)
    halves = lax.all_gather(halves, "src", axis=0, axis_index_groups=pairs)
    smem = pl.BlockSpec(memory_space=pltpu.SMEM)
    vmem = pl.BlockSpec(memory_space=pltpu.VMEM)
    wide = (src_count, LANES)
    targets, scale, lanes = pl.pallas_call(
        target_kernel,
        in_specs=[smem] + [vmem] * 3,
        out_specs=[vmem] * 3,
        out_shape=[
            jax.ShapeDtypeStruct((source.shape[0], tgt_count), jnp.bfloat16),
            jax.ShapeDtypeStruct((1, tgt_count), jnp.float32),
            jax.ShapeDtypeStruct(wide, jnp.int32),
        ],
        compiler_params=pltpu.CompilerParams(vmem_limit_bytes=32 * 1024 * 1024),
        cost_estimate=pl.CostEstimate(flops=1_000_000, bytes_accessed=2**20, transcendentals=256),
    )(starts, halves, src_near.T, tgt_near.T)
    cosines, sums = pl.pallas_call(
        functools.partial(tile_kernel, near_count),
        in_specs=[vmem] * 4,
        out_specs=[vmem] * 2,
        out_shape=[
            jax.ShapeDtypeStruct((src_count, tgt_count), jnp.float32),
            jax.ShapeDtypeStruct((2, src_count), jnp.float32),
        ],
        compiler_params=pltpu.CompilerParams(vmem_limit_bytes=32 * 1024 * 1024),
        cost_estimate=pl.CostEstimate(flops=300_000_000, bytes_accessed=2**21, transcendentals=512),
    )(source, targets, scale, lanes)

    by_rows = core == 1
    both = lax.all_gather(sums, "src", axis=0, axis_index_groups=pairs)
    sums = jnp.where(by_rows, both[:, 0], jnp.broadcast_to(jnp.sum(both[:, 1], axis=0), (2, tgt_count)))
    parts = lax.all_to_all(spread(sums, chips), ("src", "tgt"), 0, 0, axis_index_groups=lines)
    averages = jnp.sum(parts, axis=0) / near_count
    both = lax.all_gather(averages, "src", axis=0, axis_index_groups=pairs)
    margin, src_average, tgt_average = pl.pallas_call(
        margin_kernel,
        in_specs=[smem] + [vmem] * 2,
        out_specs=[vmem] * 3,
        out_shape=[
            jax.ShapeDtypeStruct((src_count, tgt_count), jnp.bfloat16),
            jax.ShapeDtypeStruct((1, src_count), jnp.float32),
            jax.ShapeDtypeStruct((1, tgt_count), jnp.float32),
        ],
        compiler_params=pltpu.CompilerParams(vmem_limit_bytes=8 * 1024 * 1024),
        cost_estimate=pl.CostEstimate(flops=200_000, bytes_accessed=2**19, transcendentals=0),
    )(core.astype(jnp.int32).reshape(1), both, cosines)
    return (margin, src_average.reshape(src_count), tgt_average.reshape(tgt_count))


def solution(mesh):
    placed = (P("src", "tgt"), P("tgt", "src"), P("src", None), P("tgt", None))
    return jax.shard_map(
        local,
        mesh=mesh,
        in_specs=placed,
        out_specs=(P("src", "tgt"), P("src"), P("tgt")),
        check_vma=False,
    )
```
